32 devices in a mesh: px: 8 (over y, x, core), py: 4 (over z).
Axes of the slice: x: 2, y: 2, z: 4, core: 2. Of those that a mesh axis runs over, the one named last changes fastest.
Arguments:
- velocity: float32 [2, 64, 16, 1024], P(None, None, 'py', 'px'), may hold values from -15 to 15
- pressure: float32 [64, 16, 1024], P(None, 'py', 'px'), may hold values from -6 to 6
- mass: bfloat16 [64, 16, 1024], P(None, 'py', 'px'), may hold values from 0.049804688 to 0.5
- face_coeff: bfloat16 [2, 64, 16, 1024], P(None, None, 'py', 'px'), may hold values from 0.29882812 to 3
- vert_coeff: bfloat16 [63, 16, 1024], P(None, 'py', 'px'), may hold values from 1 to 20
- block_inverse: bfloat16 [4, 64, 16, 1024], P(None, None, 'py', 'px'), may hold values from -0.020019531 to 0.080078125
- orientation: int32 [2, 16, 1024], P(None, 'py', 'px'), may hold values from 0 to 1
Outputs:
- new_pressure: float32 [64, 16, 1024], P(None, 'py', 'px')
- new_velocity: float32 [2, 64, 16, 1024], P(None, None, 'py', 'px')
The draws below stay inside these ranges and needn't reach their ends.
All inputs are finite; a program needn't handle non-finite values.
Results may differ from the reference program's by a relative error of at most 0.0003.
Values sent between devices are 32-bit elements; how exact they have to be, the bound alone decides.
A program may use at most 64 MiB of HBM per device.

```python
import math
import jax
import jax.numpy as jnp

LEVELS = 64
BLOCK = 4
ITERS = 4
OUTER = 2
NX = 1024
NY = 16


def draw_velocity(key, part):
    key = jax.random.fold_in(key, 11)
    column_pos = jnp.arange(NX, dtype=jnp.float32)
    x_ramp = 1.0 + 2.0 * column_pos / max(NX - 1, 1)
    full_shape = (2, LEVELS, NY, NX)
    drawn = jnp.clip(jax.random.normal(key, full_shape, jnp.float32), -5.0, 5.0) * x_ramp
    return drawn.astype(jnp.float32)


def draw_block_inverse(key, part):
    key = jax.random.fold_in(key, 23)
    first_key, second_key = jax.random.split(key)
    full_shape = (BLOCK, LEVELS, NY, NX)
    row_place = jnp.arange(LEVELS) % BLOCK
    entry_place = jnp.arange(BLOCK)
    on_diag = (entry_place[:, None] == row_place[None, :]).astype(jnp.float32)[:, :, None, None]
    diag_value = jax.random.uniform(first_key, full_shape, jnp.float32, 0.02, 0.08)
    off_diag = jax.random.uniform(second_key, full_shape, jnp.float32, -0.02, 0.02)
    drawn = on_diag * diag_value + (1.0 - on_diag) * off_diag
    return drawn.astype(jnp.bfloat16)


def place_ends(array, own_key, low, high):
    place = [jax.random.randint(jax.random.fold_in(own_key, axis), (), 0, length) for axis, length in enumerate(array.shape)]
    main_axis = array.shape.index(max(array.shape))
    neighbour = place[:main_axis] + [(place[main_axis] + 1) % array.shape[main_axis]] + place[main_axis + 1:]
    return array.at[tuple(place)].set(low).at[tuple(neighbour)].set(high)


def levels(own_key, shape, shards, least, top_value):
    factor_of, own = 1.0, jax.random.fold_in(own_key, 6)
    for dim, shards_of in shards:
        heights = jnp.exp(jax.random.uniform(jax.random.fold_in(own, dim), (shards_of,), jnp.float32, least / len(shards), top_value / len(shards)))
        factor_of = factor_of * jnp.repeat(heights, shape[dim] // shards_of).reshape([-1 if axis == dim else 1 for axis in range(len(shape))])
    return factor_of


def normal_values(rng, extent, width, bound, cuts=(), kind=jnp.bfloat16):
    array = width * jax.random.normal(rng, extent, jnp.float32)
    if cuts:
        array = array * levels(rng, extent, cuts, -0.22, 0.18)
    return jnp.clip(array, -bound, bound).astype(kind)


def setup_inputs(seed: int = 0) -> dict:
    seeds = jax.random.split(jax.random.key(seed), 8)
    return {
        "velocity": draw_velocity(jax.random.fold_in(seeds[7], 71), 0),
        "pressure": normal_values(seeds[1], (LEVELS, NY, NX), 1.0, 6.0, ((1, 4), (2, 8)), jnp.float32),
        "mass": jnp.clip(jnp.exp(math.log(0.5) - 2.306499 * jax.random.uniform(seeds[2], (LEVELS, NY, NX), jnp.float32) ** levels(seeds[2], (LEVELS, NY, NX), ((1, 4), (2, 8)), -0.2, 0.2)), 0.049804688, 0.5).astype(jnp.bfloat16),
        "face_coeff": jnp.clip(jnp.exp(math.log(3.0) - 2.306499 * jax.random.uniform(seeds[3], (2, LEVELS, NY, NX), jnp.float32) ** levels(seeds[3], (2, LEVELS, NY, NX), ((2, 4), (3, 8)), -0.2, 0.2)), 0.29882812, 3.0).astype(jnp.bfloat16),
        "vert_coeff": jnp.clip(jnp.exp(math.log(20.0) - 2.9957323 * jax.random.uniform(seeds[4], (LEVELS - 1, NY, NX), jnp.float32) ** levels(seeds[4], (LEVELS - 1, NY, NX), ((1, 4), (2, 8)), -0.2, 0.2)), 1.0, 20.0).astype(jnp.bfloat16),
        "block_inverse": draw_block_inverse(jax.random.fold_in(seeds[7], 71), 0),
        "orientation": place_ends(jax.random.randint(seeds[6], (2, NY, NX), 0, 2), jax.random.fold_in(seeds[6], 1), 0, 1).astype(jnp.int32),
    }


def from_below(values):
    return jnp.pad(values[:, :-1], ((0, 0), (1, 0), (0, 0)))


def from_above(values):
    return jnp.pad(values[:, 1:], ((0, 0), (0, 1), (0, 0)))


def operate(values, mass_f, east_coef, north_coef, vert_coef):
    east_cell = jnp.roll(values, -1, axis=2)
    west_cell = jnp.roll(values, 1, axis=2)
    north_cell = from_above(values)
    south_cell = from_below(values)
    west_coef = jnp.roll(east_coef, 1, axis=2)
    south_coef = from_below(north_coef)
    horizontal = east_coef * (values - east_cell) + west_coef * (values - west_cell) + north_coef * (values - north_cell) + south_coef * (values - south_cell)
    upper_coef = jnp.pad(vert_coef, ((0, 1), (0, 0), (0, 0)))
    lower_coef = jnp.pad(vert_coef, ((1, 0), (0, 0), (0, 0)))
    above_cell = jnp.pad(values[1:], ((0, 1), (0, 0), (0, 0)))
    below_cell = jnp.pad(values[:-1], ((1, 0), (0, 0), (0, 0)))
    vertical = upper_coef * (values - above_cell) + lower_coef * (values - below_cell)
    return mass_f * values + horizontal + vertical


def precondition(residual, block_inverse):
    block_count = residual.shape[0] // BLOCK
    blocks = residual.reshape((block_count, BLOCK) + residual.shape[1:])
    summed = jnp.zeros_like(blocks)
    for member in range(BLOCK):
        summed = summed + block_inverse[member].astype(jnp.float32).reshape(blocks.shape) * blocks[:, member:member + 1]
    return summed.reshape(residual.shape)


def reference(velocity, pressure, mass, face_coeff, vert_coeff, block_inverse, orientation):
    sign_flip = (2 * orientation - 1).astype(jnp.float32)
    mass_f = mass.astype(jnp.float32)
    east_coef = face_coeff[0].astype(jnp.float32)
    north_coef = face_coeff[1].astype(jnp.float32)
    vert_coef = vert_coeff.astype(jnp.float32)
    inverse_f = block_inverse.astype(jnp.float32)
    current = pressure
    flow = velocity
    for outer_step in range(OUTER):
        east_flux = sign_flip[0] * flow[0]
        north_flux = sign_flip[1] * flow[1]
        divergence = east_flux - jnp.roll(east_flux, 1, axis=2) + north_flux - from_below(north_flux)
        right_side = mass_f * current - divergence
        residual = right_side - operate(current, mass_f, east_coef, north_coef, vert_coef)
        searches = []
        images = []
        image_norms = []
        for inner_step in range(ITERS):
            search = precondition(residual, inverse_f)
            image = operate(search, mass_f, east_coef, north_coef, vert_coef)
            weights_proj = [jnp.sum(image * images[member]) / image_norms[member] for member in range(inner_step)]
            for member in range(inner_step):
                search = search - weights_proj[member] * searches[member]
                image = image - weights_proj[member] * images[member]
            image_norm = jnp.sum(image * image)
            step_size = jnp.sum(residual * image) / image_norm
            current = current + step_size * search
            residual = residual - step_size * image
            searches.append(search)
            images.append(image)
            image_norms.append(image_norm)
        east_cell = jnp.roll(current, -1, axis=2)
        north_cell = from_above(current)
        flow = jnp.stack([flow[0] + sign_flip[0] * east_coef * (current - east_cell), flow[1] + sign_flip[1] * north_coef * (current - north_cell)])
    return current, flow
```

```python
import functools

import jax
import jax.numpy as jnp
from jax import lax
from jax.experimental import pallas as pl
from jax.experimental.pallas import tpu as pltpu
from jax.sharding import PartitionSpec as P

BLOCK = 4
ITERS = 4
OUTER = 2
SHIFT = 3.0
MESH = pl.DeviceIdType.MESH


def solve(gram, right):
    size = len(right)
    gram = [row[:] for row in gram]
    right = right[:]
    first = [gram[i][i] for i in range(size)]
    inverse = []
    for k in range(size):
        inverse.append(jnp.where(gram[k][k] > 1e-7 * first[k], 1.0 / gram[k][k], 0.0))
        for i in range(k + 1, size):
            factor = gram[k][i] * inverse[k]
            for j in range(i, size):
                gram[i][j] = gram[i][j] - factor * gram[k][j]
            right[i] = right[i] - factor * right[k]
    weights = [None] * size
    for k in reversed(range(size)):
        total = right[k]
        for j in range(k + 1, size):
            total = total - gram[k][j] * weights[j]
        weights[k] = total * inverse[k]
    return weights


def kernel(
    npx, npy, ny, nb, nx,
    vel_ref, pres_ref, mass_ref, face_ref, vert_ref, inv_ref, orient_ref,
    p_out, u_out,
    wide, mass, ce, cw, cn, cs, wu, wl, xc, binv, prs, fe, fn, fwx, fs, res,
    W, V, seam, hs, hn, hs0, pk, xw, xe, pk0, xw0, red,
    send_y, recv_y, send_x, recv_x, send_r, recv_r,
):
    levels = BLOCK * nb
    tiles = levels // 8
    count = npx * npy
    px, py = lax.axis_index("px"), lax.axis_index("py")
    east, west = lax.rem(px + 1, npx), lax.rem(px + npx - 1, npx)
    has_north, has_south = py < npy - 1, py > 0
    me = px * npy + py

    barrier = pltpu.get_barrier_semaphore()

    def partner(step):
        other = lax.rem(me + step, count)
        return (lax.div(other, npy), lax.rem(other, npy))

    def greet(step, carry):
        pl.semaphore_signal(barrier, inc=1, device_id=partner(step), device_id_type=MESH)
        return carry

    lax.fori_loop(1, count, greet, 0)

    def gather(ref, base, y):
        return jnp.concatenate(
            [
                ref[pl.ds(base + m * ny + y, nb, stride=BLOCK * ny), :]
                for m in range(BLOCK)
            ],
            axis=0,
        )

    def scatter(ref, base, y, value):
        for m in range(BLOCK):
            ref[pl.ds(base + m * ny + y, nb, stride=BLOCK * ny), :] = value[m * nb : (m + 1) * nb]

    lane = lax.broadcasted_iota(jnp.int32, (8, nx), 1)
    lane_l = lax.broadcasted_iota(jnp.int32, (levels, nx), 1)
    even = lax.rem(lane, 2) == 0

    def pack(slabs):
        total = jnp.zeros((8, nx), jnp.float32)
        for y in range(ny):
            for t in range(tiles):
                i = y * tiles + t
                turned = slabs[y][t * 8 : (t + 1) * 8]
                if i:
                    turned = pltpu.roll(turned, 2 * i, axis=1)
                mine = (lane == 2 * i) | (lane == (2 * i - 1) % nx)
                total = jnp.where(mine, turned, total)
        return total

    def meet(from_west, from_east):
        return jnp.where(even, pltpu.roll(from_west, 1, axis=1), pltpu.roll(from_east, nx - 1, axis=1))

    def spread(packed, y):
        parts = []
        for t in range(tiles):
            i = y * tiles + t
            parts.append(pltpu.roll(packed, nx - 2 * i, axis=1) if i else packed)
        return jnp.concatenate(parts, axis=0)

    def up(slab):
        return jnp.concatenate([slab[nb:], pltpu.roll(slab[:nb], nb - 1, axis=0)], axis=0)

    def down(slab):
        return jnp.concatenate([pltpu.roll(slab[levels - nb :], 1, axis=0), slab[: levels - nb]], axis=0)

    def roll_w(slab):
        return pltpu.roll(slab, 1, axis=1)

    def roll_e(slab):
        return pltpu.roll(slab, nx - 1, axis=1)

    def y_copies(low, high, low_dst, high_dst, k):
        north = pltpu.make_async_remote_copy(
            src_ref=high, dst_ref=high_dst, send_sem=send_y.at[k, 0], recv_sem=recv_y.at[k, 0],
            device_id=(px, py + 1), device_id_type=MESH)
        south = pltpu.make_async_remote_copy(
            src_ref=low, dst_ref=low_dst, send_sem=send_y.at[k, 1], recv_sem=recv_y.at[k, 1],
            device_id=(px, py - 1), device_id_type=MESH)
        return north, south

    def x_copies(to_east, to_west, east_dst, west_dst, k):
        a = pltpu.make_async_remote_copy(
            src_ref=to_east, dst_ref=east_dst, send_sem=send_x.at[k, 0], recv_sem=recv_x.at[k, 0],
            device_id=(east, py), device_id_type=MESH)
        b = pltpu.make_async_remote_copy(
            src_ref=to_west, dst_ref=west_dst, send_sem=send_x.at[k, 1], recv_sem=recv_x.at[k, 1],
            device_id=(west, py), device_id_type=MESH)
        return a, b

    def start(copies):
        (north, south), (a, b) = copies

        @pl.when(has_north)
        def _():
            north.start()

        @pl.when(has_south)
        def _():
            south.start()

        a.start()
        b.start()

    def finish(copies):
        (north, south), (a, b) = copies
        a.wait_recv()
        b.wait_recv()

        @pl.when(has_south)
        def _():
            north.wait_recv()

        @pl.when(has_north)
        def _():
            south.wait_recv()

    def sent(copies):
        (north, south), (a, b) = copies
        a.wait_send()
        b.wait_send()

        @pl.when(has_north)
        def _():
            north.wait_send()

        @pl.when(has_south)
        def _():
            south.wait_send()

    wide[0] = face_ref[0 : levels * ny].astype(jnp.float32)
    wide[1] = face_ref[levels * ny :].astype(jnp.float32)
    sign = 2.0 * orient_ref[...].astype(jnp.float32) - 1.0
    for y in range(ny):
        ce[y] = gather(wide.at[0], 0, y)
        cn[y] = gather(wide.at[1], 0, y)
        prs[y] = gather(pres_ref, 0, y)
        fe[y] = sign[y : y + 1] * gather(vel_ref, 0, y)
        fn[y] = sign[ny + y : ny + y + 1] * gather(vel_ref, levels * ny, y)
    seam[0] = prs[ny - 1]
    seam[1] = fn[ny - 1]
    seam[2] = cn[ny - 1]
    pk0[0] = pack(prs)
    pk0[1] = pack(fe)
    pk0[2] = pack(ce)

    @pl.when(jnp.logical_not(has_south))
    def _():
        hs0[...] = jnp.zeros_like(hs0)
        hs[...] = jnp.zeros_like(hs)

    @pl.when(jnp.logical_not(has_north))
    def _():
        hn[...] = jnp.zeros_like(hn)

    pl.semaphore_wait(barrier, count - 1)

    first = (
        y_copies(prs.at[0], seam, hn.at[0], hs0, 0),
        x_copies(pk0, pk0.at[0], xw0, xe.at[0], 0),
    )
    start(first)

    wide[0] = mass_ref[...].astype(jnp.float32)
    wide[1] = jnp.zeros_like(wide[1])
    wide[1, 0 : (levels - 1) * ny, :] = vert_ref[...].astype(jnp.float32)
    for j in range(BLOCK):
        wide[2 + j] = inv_ref[j * levels * ny : (j + 1) * levels * ny].astype(jnp.float32)
    for y in range(ny):
        mass[y] = gather(wide.at[0], 0, y)
        slab = gather(wide.at[1], 0, y)
        wu[y] = slab
        wl[y] = down(slab)
        for j in range(BLOCK):
            binv[j, y] = gather(wide.at[2 + j], 0, y)

    finish(first)
    sent(first)
    packed_c = meet(xw0[2], xw0[2])
    packed_f = meet(xw0[1], xw0[1])
    for y in range(ny):
        left = jnp.where(lane_l == 0, spread(packed_c, y), roll_w(ce[y]))
        cw[y] = left
        cs[y] = hs0[2] if y == 0 else cn[y - 1]
        xc[y] = jnp.where(lane_l == 0, left, jnp.where(lane_l == nx - 1, ce[y], 0.0))
        fwx[y] = spread(packed_f, y)
    fs[...] = hs0[1]

    def inside(values, y):
        v = values[y]
        to_east = jnp.where(lane_l == nx - 1, 0.0, roll_e(v))
        to_west = jnp.where(lane_l == 0, 0.0, roll_w(v))
        total = mass[y] * v + ce[y] * (v - to_east) + cw[y] * (v - to_west)
        total += cn[y] * (v - values[y + 1]) if y < ny - 1 else cn[y] * v
        total += cs[y] * (v - values[y - 1]) if y > 0 else cs[y] * v
        return total + wu[y] * (v - up(v)) + wl[y] * (v - down(v))

    def rim(y, packed, south, north):
        total = xc[y] * spread(packed, y)
        if y == 0:
            total += cs[y] * south
        if y == ny - 1:
            total += cn[y] * north
        return total

    def precondition(blocks, y):
        parts = []
        for m in range(BLOCK):
            rows = slice(m * nb, (m + 1) * nb)
            total = binv[0, y, rows] * blocks[0:nb]
            for j in range(1, BLOCK):
                total += binv[j, y, rows] * blocks[j * nb : (j + 1) * nb]
            parts.append(total)
        return jnp.concatenate(parts, axis=0)

    def fold(slab):
        total = slab[0:8]
        for t in range(1, tiles):
            total += slab[t * 8 : (t + 1) * 8]
        return total

    p_south, p_north = hs0[0], hn[0]
    p_packed = meet(xw0[0], xe[0])

    for outer in range(OUTER):
        for y in range(ny):
            f_west = jnp.where(lane_l == 0, fwx[y], roll_w(fe[y]))
            f_south = fs[...] if y == 0 else fn[y - 1]
            div = fe[y] - f_west + fn[y] - f_south
            image = inside(prs, y) - rim(y, p_packed, p_south, p_north)
            residual = mass[y] * prs[y] - div - image
            res[y] = residual
            W[0, y] = precondition(residual, y)
        packs = []
        souths, norths = [], []
        dots = {}
        for i in range(ITERS):
            k = 1 + outer * ITERS + i
            pk[k - 1] = pack([W[i, y] for y in range(ny)])
            for_y = y_copies(W.at[i, 0], W.at[i, ny - 1], hn.at[k], hs.at[k - 1], k)
            copies = (for_y, x_copies(pk.at[k - 1], pk.at[k - 1], xw.at[k - 1], xe.at[k], k))
            start(copies)
            for y in range(ny):
                V[i, y] = inside(W.at[i], y)
            if i > 0:
                for j in range(i):
                    dots[j, i - 1] = sum(fold(V[j, y] * V[i - 1, y]) for y in range(ny))
                dots["r", i - 1] = sum(fold(res[y] * V[i - 1, y]) for y in range(ny))
            finish(copies)
            packed = meet(xw[k - 1], xe[k])
            packs.append(packed)
            for y in range(ny):
                image = V[i, y] - rim(y, packed, hs[k - 1], hn[k])
                V[i, y] = image
                if i < ITERS - 1:
                    W[i + 1, y] = precondition(image, y) - SHIFT * W[i, y]
            sent(copies)
        last = ITERS - 1
        for j in range(ITERS):
            dots[j, last] = sum(fold(V[j, y] * V[last, y]) for y in range(ny))
        dots["r", last] = sum(fold(res[y] * V[last, y]) for y in range(ny))

        order = [(j, i) for i in range(ITERS) for j in range(i + 1)]
        order += [("r", i) for i in range(ITERS)]
        rows = [jnp.sum(dots[key], axis=0, keepdims=True) for key in order]
        rows += [jnp.zeros_like(rows[0])] * (16 - len(rows))
        low, high = jnp.concatenate(rows[:8], axis=0), jnp.concatenate(rows[8:], axis=0)
        half = nx // 2
        low += pltpu.roll(low, half, axis=1)
        high += pltpu.roll(high, half, axis=1)
        red[outer, me] = jnp.where(lane < half, low, high)

        def share(step, carry):
            pltpu.make_async_remote_copy(
                src_ref=red.at[outer, me], dst_ref=red.at[outer, me],
                send_sem=send_r.at[outer], recv_sem=recv_r.at[outer],
                device_id=partner(step), device_id_type=MESH).start()
            return carry

        lax.fori_loop(1, count, share, 0)
        rest = red.at[outer, pl.ds(0, count - 1)]
        pltpu.make_async_copy(rest, rest, recv_r.at[outer]).wait()
        pltpu.make_async_copy(rest, rest, send_r.at[outer]).wait()
        total = jnp.sum(red[outer], axis=0)
        low = jnp.sum(jnp.where(lane < half, total, 0.0), axis=1, keepdims=True)
        high = jnp.sum(jnp.where(lane < half, 0.0, total), axis=1, keepdims=True)
        sums = {}
        for n, key in enumerate(order):
            column = low if n < 8 else high
            sums[key] = jnp.broadcast_to(column[n % 8 : n % 8 + 1], (8, nx))
        gram = [[sums[min(i, j), max(i, j)] for j in range(ITERS)] for i in range(ITERS)]
        weights = solve(gram, [sums["r", i] for i in range(ITERS)])
        wide_weights = [jnp.broadcast_to(c[0:1], (levels, nx)) for c in weights]

        for i in range(ITERS):
            k = 1 + outer * ITERS + i
            p_packed += weights[i] * packs[i]
            p_south += wide_weights[i] * hs[k - 1]
            p_north += wide_weights[i] * hn[k]
        for y in range(ny):
            value = prs[y]
            for i in range(ITERS):
                value += wide_weights[i] * W[i, y]
            prs[y] = value
        for y in range(ny):
            value = prs[y]
            edge = spread(p_packed, y)
            to_east = jnp.where(lane_l == nx - 1, edge, roll_e(value))
            to_north = prs[y + 1] if y < ny - 1 else p_north
            fe[y] = fe[y] + ce[y] * (value - to_east)
            fn[y] = fn[y] + cn[y] * (value - to_north)
            if outer < OUTER - 1:
                fwx[y] = fwx[y] + cw[y] * (edge - value)
                if y == 0:
                    fs[...] = fs[...] + cs[0] * (p_south - value)
            else:
                scatter(p_out, 0, y, value)
                scatter(u_out, 0, y, sign[y : y + 1] * fe[y])
                scatter(u_out, levels * ny, y, sign[ny + y : ny + y + 1] * fn[y])


def local(npx, npy, velocity, pressure, mass, face_coeff, vert_coeff, block_inverse, orientation):
    levels, ny, nx = pressure.shape
    nb = levels // BLOCK
    f32 = jnp.float32
    rounds = OUTER * ITERS
    field = pltpu.VMEM((ny, levels, nx), f32)
    slab = pltpu.VMEM((levels, nx), f32)
    inputs = [a.reshape(-1, nx) for a in (velocity, pressure, mass, face_coeff, vert_coeff, block_inverse, orientation)]
    vmem = pl.BlockSpec(memory_space=pltpu.VMEM)
    scratch = dict(
        wide=pltpu.VMEM((2 + BLOCK, levels * ny, nx), f32),
        mass=field, ce=field, cw=field, cn=field, cs=field, wu=field, wl=field, xc=field,
        binv=pltpu.VMEM((BLOCK, ny, levels, nx), f32),
        prs=field, fe=field, fn=field, fwx=field, fs=slab, res=field,
        W=pltpu.VMEM((ITERS, ny, levels, nx), f32),
        V=pltpu.VMEM((ITERS, ny, levels, nx), f32),
        seam=pltpu.VMEM((3, levels, nx), f32),
        hs=pltpu.VMEM((rounds, levels, nx), f32),
        hn=pltpu.VMEM((rounds + 1, levels, nx), f32),
        hs0=pltpu.VMEM((3, levels, nx), f32),
        pk=pltpu.VMEM((rounds, 8, nx), f32),
        xw=pltpu.VMEM((rounds, 8, nx), f32),
        xe=pltpu.VMEM((rounds + 1, 8, nx), f32),
        pk0=pltpu.VMEM((3, 8, nx), f32),
        xw0=pltpu.VMEM((3, 8, nx), f32),
        red=pltpu.VMEM((OUTER, npx * npy, 8, nx), f32),
        send_y=pltpu.SemaphoreType.DMA((rounds + 1, 2)),
        recv_y=pltpu.SemaphoreType.DMA((rounds + 1, 2)),
        send_x=pltpu.SemaphoreType.DMA((rounds + 1, 2)),
        recv_x=pltpu.SemaphoreType.DMA((rounds + 1, 2)),
        send_r=pltpu.SemaphoreType.DMA((OUTER,)),
        recv_r=pltpu.SemaphoreType.DMA((OUTER,)),
    )
    p_new, u_new = pl.pallas_call(
        functools.partial(kernel, npx, npy, ny, nb, nx),
        out_shape=(
            jax.ShapeDtypeStruct((levels * ny, nx), f32),
            jax.ShapeDtypeStruct((2 * levels * ny, nx), f32),
        ),
        in_specs=[vmem] * 7,
        out_specs=(vmem, vmem),
        scratch_shapes=list(scratch.values()),
        compiler_params=pltpu.CompilerParams(
            collective_id=0, has_side_effects=True, vmem_limit_bytes=40 * 1024 * 1024
        ),
    )(*inputs)
    return p_new.reshape(pressure.shape), u_new.reshape(velocity.shape)


def solution(mesh):
    placed = (
        P(None, None, "py", "px"),
        P(None, "py", "px"),
        P(None, "py", "px"),
        P(None, None, "py", "px"),
        P(None, "py", "px"),
        P(None, None, "py", "px"),
        P(None, "py", "px"),
    )
    return jax.shard_map(
        functools.partial(local, mesh.shape["px"], mesh.shape["py"]),
        mesh=mesh,
        in_specs=placed,
        out_specs=(P(None, "py", "px"), P(None, None, "py", "px")),
        check_vma=False,
    )
```

```python
import functools

import jax
import jax.numpy as jnp
from jax import lax
from jax.experimental import pallas as pl
from jax.experimental.pallas import tpu as pltpu
from jax.sharding import PartitionSpec as P

BLOCK = 4
ITERS = 4
OUTER = 2
SHIFT = 3.0
MESH = pl.DeviceIdType.MESH


def solve(gram, right):
    size = len(right)
    gram = [row[:] for row in gram]
    right = right[:]
    first = [gram[i][i] for i in range(size)]
    inverse = []
    for k in range(size):
        inverse.append(jnp.where(gram[k][k] > 1e-7 * first[k], 1.0 / gram[k][k], 0.0))
        for i in range(k + 1, size):
            factor = gram[k][i] * inverse[k]
            for j in range(i, size):
                gram[i][j] = gram[i][j] - factor * gram[k][j]
            right[i] = right[i] - factor * right[k]
    weights = [None] * size
    for k in reversed(range(size)):
        total = right[k]
        for j in range(k + 1, size):
            total = total - gram[k][j] * weights[j]
        weights[k] = total * inverse[k]
    return weights


def kernel(
    npx, npy, ny, nb, nx,
    vel_hbm, pres_hbm, mass_hbm, face_hbm, vert_hbm, inv_hbm, orient_hbm,
    p_out, u_out,
    vel_ref, pres_ref, mass_ref, face_ref, vert_ref, inv_ref, orient_ref,
    wide, wide_w, mass, ce, cw, cn, cs, wu, wl, xc, binv, prs, fe, fn, res, G, MG, gs, gn, gpk, gxw, gxe,
    W, V, low_p, seam, hs, hn, hs0, pk, xw, xe, pk0, xw0, red,
    send_y, recv_y, send_x, recv_x, send_r, recv_r, fetch,
):
    levels = BLOCK * nb
    tiles = levels // 8
    count = npx * npy
    px, py = lax.axis_index("px"), lax.axis_index("py")
    east, west = lax.rem(px + 1, npx), lax.rem(px + npx - 1, npx)
    has_north, has_south = py < npy - 1, py > 0
    me = px * npy + py

    barrier = pltpu.get_barrier_semaphore()

    partners = [
        (lax.rem(px + i, npx), lax.rem(py + j, npy))
        for i in range(npx) for j in range(npy) if i or j
    ]
    for target in partners:
        pl.semaphore_signal(barrier, inc=1, device_id=target, device_id_type=MESH)

    fetches = [
        pltpu.make_async_copy(src, dst, fetch.at[n])
        for n, (src, dst) in enumerate([
            (face_hbm, face_ref), (pres_hbm, pres_ref), (vel_hbm, vel_ref), (orient_hbm, orient_ref),
            (mass_hbm, mass_ref), (vert_hbm, vert_ref), (inv_hbm, inv_ref),
        ])
    ]
    for copy in fetches:
        copy.start()

    def gather(ref, base, y):
        return jnp.concatenate(
            [
                ref[pl.ds(base + m * ny + y, nb, stride=BLOCK * ny), :]
                for m in range(BLOCK)
            ],
            axis=0,
        )

    def scatter(ref, base, y, value):
        for m in range(BLOCK):
            ref[pl.ds(base + m * ny + y, nb, stride=BLOCK * ny), :] = value[m * nb : (m + 1) * nb]

    lane = lax.broadcasted_iota(jnp.int32, (8, nx), 1)
    lane_l = lax.broadcasted_iota(jnp.int32, (levels, nx), 1)
    even = lax.rem(lane, 2) == 0
    lane_16 = lax.broadcasted_iota(jnp.int32, (16, nx), 1)
    group = lax.broadcasted_iota(jnp.int32, (16, nx), 0)

    def pack(slabs):
        total = jnp.zeros((8, nx), jnp.float32)
        for y in range(ny):
            for t in range(tiles):
                i = y * tiles + t
                turned = slabs[y][t * 8 : (t + 1) * 8]
                if i:
                    turned = pltpu.roll(turned, 2 * i, axis=1)
                mine = (lane == 2 * i) | (lane == (2 * i - 1) % nx)
                total = jnp.where(mine, turned, total)
        return total

    def meet(from_west, from_east):
        return jnp.where(even, pltpu.roll(from_west, 1, axis=1), pltpu.roll(from_east, nx - 1, axis=1))

    def spread(packed, y):
        parts = []
        for t in range(tiles):
            i = y * tiles + t
            parts.append(pltpu.roll(packed, nx - 2 * i, axis=1) if i else packed)
        return jnp.concatenate(parts, axis=0)

    def up(slab):
        return jnp.concatenate([slab[nb:], pltpu.roll(slab[:nb], nb - 1, axis=0)], axis=0)

    def down(slab):
        return jnp.concatenate([pltpu.roll(slab[levels - nb :], 1, axis=0), slab[: levels - nb]], axis=0)

    def roll_w(slab):
        return pltpu.roll(slab, 1, axis=1)

    def roll_e(slab):
        return pltpu.roll(slab, nx - 1, axis=1)

    def y_copies(low, high, low_dst, high_dst, k):
        north = pltpu.make_async_remote_copy(
            src_ref=high, dst_ref=high_dst, send_sem=send_y.at[k, 0], recv_sem=recv_y.at[k, 0],
            device_id=(px, py + 1), device_id_type=MESH)
        south = pltpu.make_async_remote_copy(
            src_ref=low, dst_ref=low_dst, send_sem=send_y.at[k, 1], recv_sem=recv_y.at[k, 1],
            device_id=(px, py - 1), device_id_type=MESH)
        return north, south

    def x_copies(to_east, to_west, east_dst, west_dst, k):
        a = pltpu.make_async_remote_copy(
            src_ref=to_east, dst_ref=east_dst, send_sem=send_x.at[k, 0], recv_sem=recv_x.at[k, 0],
            device_id=(east, py), device_id_type=MESH)
        b = pltpu.make_async_remote_copy(
            src_ref=to_west, dst_ref=west_dst, send_sem=send_x.at[k, 1], recv_sem=recv_x.at[k, 1],
            device_id=(west, py), device_id_type=MESH)
        return a, b

    def start(copies):
        (north, south), (a, b) = copies

        @pl.when(has_north)
        def _():
            north.start()

        @pl.when(has_south)
        def _():
            south.start()

        a.start()
        b.start()

    def finish(copies):
        (north, south), (a, b) = copies
        a.wait_recv()
        b.wait_recv()

        @pl.when(has_south)
        def _():
            north.wait_recv()

        @pl.when(has_north)
        def _():
            south.wait_recv()

    def sent(copies):
        (north, south), (a, b) = copies
        a.wait_send()
        b.wait_send()

        @pl.when(has_north)
        def _():
            north.wait_send()

        @pl.when(has_south)
        def _():
            south.wait_send()

    for copy in fetches[:4]:
        copy.wait()
    wide[0] = face_ref[0 : levels * ny].astype(jnp.float32)
    wide[1] = face_ref[levels * ny :].astype(jnp.float32)
    sign = 2.0 * orient_ref[...].astype(jnp.float32) - 1.0
    for y in range(ny):
        ce[y] = gather(wide.at[0], 0, y)
        cn[y] = gather(wide.at[1], 0, y)
        prs[y] = gather(pres_ref, 0, y)
        fe[y] = sign[y : y + 1] * gather(vel_ref, 0, y)
        fn[y] = sign[ny + y : ny + y + 1] * gather(vel_ref, levels * ny, y)
    seam[0] = prs[ny - 1]
    low_p[...] = prs[0]
    seam[1] = fn[ny - 1]
    seam[2] = cn[ny - 1]
    pk0[0] = pack(prs)
    pk0[1] = pack(fe)
    pk0[2] = pack(ce)

    @pl.when(jnp.logical_not(has_south))
    def _():
        hs0[...] = jnp.zeros_like(hs0)
        hs[...] = jnp.zeros_like(hs)
        gs[...] = jnp.zeros_like(gs)

    @pl.when(jnp.logical_not(has_north))
    def _():
        hn[...] = jnp.zeros_like(hn)
        gn[...] = jnp.zeros_like(gn)

    pl.semaphore_wait(barrier, count - 1)

    first = (
        y_copies(low_p, seam, hn.at[0], hs0, 0),
        x_copies(pk0, pk0.at[0], xw0, xe.at[0], 0),
    )
    start(first)

    for copy in fetches[4:]:
        copy.wait()
    wide[0] = mass_ref[...].astype(jnp.float32)
    wide_w[0 : levels - 1] = vert_ref[...].astype(jnp.float32)
    wide_w[levels - 1] = jnp.zeros((ny, nx), jnp.float32)
    for j in range(BLOCK):
        wide[1 + j] = inv_ref[j * levels * ny : (j + 1) * levels * ny].astype(jnp.float32)
    for y in range(ny):
        mass[y] = gather(wide.at[0], 0, y)
        slab = jnp.concatenate(
            [wide_w[pl.ds(m, nb, stride=BLOCK), y, :] for m in range(BLOCK)], axis=0
        )
        wu[y] = slab
        wl[y] = down(slab)
        for j in range(BLOCK):
            binv[j, y] = gather(wide.at[1 + j], 0, y)

    finish(first)
    packed_c = meet(xw0[2], xw0[2])
    packed_f = meet(xw0[1], xw0[1])
    for y in range(ny):
        left = jnp.where(lane_l == 0, spread(packed_c, y), roll_w(ce[y]))
        cw[y] = left
        cs[y] = hs0[2] if y == 0 else cn[y - 1]
        xc[y] = jnp.where(lane_l == 0, left, jnp.where(lane_l == nx - 1, ce[y], 0.0))

    def inside(values, y):
        v = values[y]
        to_east = jnp.where(lane_l == nx - 1, 0.0, roll_e(v))
        to_west = jnp.where(lane_l == 0, 0.0, roll_w(v))
        flat = ce[y] * (v - to_east) + cw[y] * (v - to_west)
        flat += cn[y] * (v - values[y + 1]) if y < ny - 1 else cn[y] * v
        flat += cs[y] * (v - values[y - 1]) if y > 0 else cs[y] * v
        return flat, mass[y] * v + flat + wu[y] * (v - up(v)) + wl[y] * (v - down(v))

    def rim(y, packed, south, north):
        total = xc[y] * spread(packed, y)
        if y == 0:
            total += cs[y] * south
        if y == ny - 1:
            total += cn[y] * north
        return total

    def precondition(blocks, y):
        parts = []
        for m in range(BLOCK):
            rows = slice(m * nb, (m + 1) * nb)
            total = binv[0, y, rows] * blocks[0:nb]
            for j in range(1, BLOCK):
                total += binv[j, y, rows] * blocks[j * nb : (j + 1) * nb]
            parts.append(total)
        return jnp.concatenate(parts, axis=0)

    def fold(slab):
        total = slab[0:8]
        for t in range(1, tiles):
            total += slab[t * 8 : (t + 1) * 8]
        return total

    p_south, p_north = hs0[0], hn[0]
    p_packed = meet(xw0[0], xe[0])

    pending = []

    def offer(n):
        gpk[n] = pack([MG[n, y] for y in range(ny)])
        k = 1 + OUTER * ITERS + n
        copies = (
            y_copies(MG.at[n, 0], MG.at[n, ny - 1], gn.at[n], gs.at[n], k),
            x_copies(gpk.at[n], gpk.at[n], gxw.at[n], gxe.at[n], k),
        )
        start(copies)
        pending.append(copies)
        return copies

    def combine(first, terms, factors):
        for term, factor in zip(terms, factors):
            first += factor * term
        return first

    for y in range(ny):
        f_west = jnp.where(lane_l == 0, spread(packed_f, y), roll_w(fe[y]))
        f_south = hs0[1] if y == 0 else fn[y - 1]
        div = fe[y] - f_west + fn[y] - f_south
        flat, image = inside(prs, y)
        border = rim(y, p_packed, p_south, p_north)
        residual = mass[y] * prs[y] - div - (image - border)
        res[y] = residual
        W[0, y] = precondition(residual, y)
        G[ITERS, y] = residual - (flat - border)

    def update(outer, packs, souths, norths, weights, wide_weights, state):
        p_packed, p_south, p_north = state
        p_packed = combine(p_packed, packs, weights)
        p_south = combine(p_south, souths, wide_weights)
        p_north = combine(p_north, norths, wide_weights)
        for y in range(ny):
            prs[y] = combine(prs[y], [W[outer * ITERS + i, y] for i in range(ITERS)], wide_weights)
        for y in range(ny):
            value = prs[y]
            to_east = jnp.where(lane_l == nx - 1, spread(p_packed, y), roll_e(value))
            to_north = prs[y + 1] if y < ny - 1 else p_north
            fe[y] = fe[y] + ce[y] * (value - to_east)
            fn[y] = fn[y] + cn[y] * (value - to_north)
        return p_packed, p_south, p_north

    state = (p_packed, p_south, p_north)
    late = None
    offers = []
    for outer in range(OUTER):
        start_w = outer * ITERS
        packs, souths, norths = [], [], []
        dots = {}
        for i in range(ITERS):
            k = 1 + outer * ITERS + i
            ready = outer > 0 and i == 0
            if not ready:
                pk[k - 1] = pack([W[start_w + i, y] for y in range(ny)])
                copies = (
                    y_copies(W.at[start_w + i, 0], W.at[start_w + i, ny - 1], hn.at[k], hs.at[k - 1], k),
                    x_copies(pk.at[k - 1], pk.at[k - 1], xw.at[k - 1], xe.at[k], k),
                )
                start(copies)
                pending.append(copies)
            for y in range(ny):
                flat, image = inside(W.at[start_w + i], y)
                V[i, y] = image
                if outer < OUTER - 1:
                    G[i, y] = mass[y] * W[start_w + i, y] - flat - image
            if i > 0:
                for j in range(i):
                    dots[j, i - 1] = sum(fold(V[j, y] * V[i - 1, y]) for y in range(ny))
                dots["r", i - 1] = sum(fold(res[y] * V[i - 1, y]) for y in range(ny))
            if outer < OUTER - 1:
                term = (i - 1) % (ITERS + 1)
                for y in range(ny):
                    MG[term, y] = precondition(G[term, y], y)
                offers.append((term, offer(term)))
            if outer > 0 and i == 1:
                state = update(outer - 1, *late, state)
            if ready:
                packed, south, north = started
            else:
                finish(copies)
                packed, south, north = meet(xw[k - 1], xe[k]), hs[k - 1], hn[k]
            packs.append(packed)
            souths.append(south)
            norths.append(north)
            for y in range(ny):
                border = rim(y, packed, south, north)
                image = V[i, y] - border
                V[i, y] = image
                if i < ITERS - 1:
                    W[start_w + i + 1, y] = precondition(image, y) - SHIFT * W[start_w + i, y]
                if outer < OUTER - 1:
                    G[i, y] = G[i, y] + 2.0 * border
        last = ITERS - 1
        for j in range(ITERS):
            dots[j, last] = sum(fold(V[j, y] * V[last, y]) for y in range(ny))
        dots["r", last] = sum(fold(res[y] * V[last, y]) for y in range(ny))

        order = [(j, i) for i in range(ITERS) for j in range(i + 1)]
        order += [("r", i) for i in range(ITERS)]
        rows = [jnp.sum(dots[key], axis=0, keepdims=True) for key in order]
        rows += [jnp.zeros_like(rows[0])] * (16 - len(rows))
        rows = jnp.sum(jnp.concatenate(rows, axis=0), axis=1, keepdims=True)
        red[outer, me] = jnp.sum(jnp.where(group == lane_16, rows, 0.0), axis=0, keepdims=True)
        for target in partners:
            pltpu.make_async_remote_copy(
                src_ref=red.at[outer, me], dst_ref=red.at[outer, me],
                send_sem=send_r.at[outer], recv_sem=recv_r.at[outer],
                device_id=target, device_id_type=MESH).start()
        if outer < OUTER - 1:
            for y in range(ny):
                MG[last, y] = precondition(G[last, y], y)
            offers.append((last, offer(last)))
        rest = red.at[outer, pl.ds(0, count - 1)]
        pltpu.make_async_copy(rest, rest, recv_r.at[outer]).wait()
        total = jnp.sum(red[outer], axis=0)
        column = jnp.sum(jnp.where(group == lane_16, total, 0.0), axis=1, keepdims=True)
        sums = {}
        for n, key in enumerate(order):
            sums[key] = jnp.broadcast_to(column[n : n + 1], (8, nx))
        gram = [[sums[min(i, j), max(i, j)] for j in range(ITERS)] for i in range(ITERS)]
        weights = solve(gram, [sums["r", i] for i in range(ITERS)])
        wide_weights = [jnp.broadcast_to(c[0:1], (levels, nx)) for c in weights]

        late = (packs, souths, norths, weights, wide_weights)
        if outer < OUTER - 1:
            for y in range(ny):
                W[start_w + ITERS, y] = combine(MG[ITERS, y], [MG[i, y] for i in range(ITERS)], wide_weights)
                res[y] = combine(G[ITERS, y], [G[i, y] for i in range(ITERS)], wide_weights)
            for term, copies in offers:
                finish(copies)
            offers = []
            meets = [meet(gxw[i], gxe[i]) for i in range(ITERS + 1)]
            started = (
                combine(meets[ITERS], meets[:ITERS], weights),
                combine(gs[ITERS], [gs[i] for i in range(ITERS)], wide_weights),
                combine(gn[ITERS], [gn[i] for i in range(ITERS)], wide_weights),
            )
    update(OUTER - 1, *late, state)
    for y in range(ny):
        scatter(p_out, 0, y, prs[y])
        scatter(u_out, 0, y, sign[y : y + 1] * fe[y])
        scatter(u_out, levels * ny, y, sign[ny + y : ny + y + 1] * fn[y])
    sent(first)
    for copies in pending:
        sent(copies)
    for outer in range(OUTER):
        rest = red.at[outer, pl.ds(0, count - 1)]
        pltpu.make_async_copy(rest, rest, send_r.at[outer]).wait()


def local(npx, npy, velocity, pressure, mass, face_coeff, vert_coeff, block_inverse, orientation):
    levels, ny, nx = pressure.shape
    nb = levels // BLOCK
    f32 = jnp.float32
    rounds = OUTER * ITERS
    field = pltpu.VMEM((ny, levels, nx), f32)
    slab = pltpu.VMEM((levels, nx), f32)
    flat = [a.reshape(-1, nx) for a in (velocity, pressure, mass, face_coeff, block_inverse, orientation)]
    inputs = flat[:4] + [vert_coeff] + flat[4:]
    names = ("vel_ref", "pres_ref", "mass_ref", "face_ref", "vert_ref", "inv_ref", "orient_ref")
    vmem = pl.BlockSpec(memory_space=pltpu.VMEM)
    scratch = dict(
        **{name: pltpu.VMEM(a.shape, a.dtype) for name, a in zip(names, inputs)},
        wide=pltpu.VMEM((1 + BLOCK, levels * ny, nx), f32),
        wide_w=pltpu.VMEM((levels, ny, nx), f32),
        mass=field, ce=field, cw=field, cn=field, cs=field, wu=field, wl=field, xc=field,
        binv=pltpu.VMEM((BLOCK, ny, levels, nx), f32),
        prs=field, fe=field, fn=field, res=field,
        G=pltpu.VMEM((ITERS + 1, ny, levels, nx), f32),
        MG=pltpu.VMEM((ITERS + 1, ny, levels, nx), f32),
        gs=pltpu.VMEM((ITERS + 1, levels, nx), f32),
        gn=pltpu.VMEM((ITERS + 1, levels, nx), f32),
        gpk=pltpu.VMEM((ITERS + 1, 8, nx), f32),
        gxw=pltpu.VMEM((ITERS + 1, 8, nx), f32),
        gxe=pltpu.VMEM((ITERS + 1, 8, nx), f32),
        W=pltpu.VMEM((OUTER * ITERS, ny, levels, nx), f32),
        V=pltpu.VMEM((ITERS, ny, levels, nx), f32),
        low_p=slab,
        seam=pltpu.VMEM((3, levels, nx), f32),
        hs=pltpu.VMEM((rounds, levels, nx), f32),
        hn=pltpu.VMEM((rounds + 1, levels, nx), f32),
        hs0=pltpu.VMEM((3, levels, nx), f32),
        pk=pltpu.VMEM((rounds, 8, nx), f32),
        xw=pltpu.VMEM((rounds, 8, nx), f32),
        xe=pltpu.VMEM((rounds + 1, 8, nx), f32),
        pk0=pltpu.VMEM((3, 8, nx), f32),
        xw0=pltpu.VMEM((3, 8, nx), f32),
        red=pltpu.VMEM((OUTER, npx * npy, 1, nx), f32),
        send_y=pltpu.SemaphoreType.DMA((rounds + ITERS + 2, 2)),
        recv_y=pltpu.SemaphoreType.DMA((rounds + ITERS + 2, 2)),
        send_x=pltpu.SemaphoreType.DMA((rounds + ITERS + 2, 2)),
        recv_x=pltpu.SemaphoreType.DMA((rounds + ITERS + 2, 2)),
        send_r=pltpu.SemaphoreType.DMA((OUTER,)),
        recv_r=pltpu.SemaphoreType.DMA((OUTER,)),
        fetch=pltpu.SemaphoreType.DMA((7,)),
    )
    p_new, u_new = pl.pallas_call(
        functools.partial(kernel, npx, npy, ny, nb, nx),
        out_shape=(
            jax.ShapeDtypeStruct((levels * ny, nx), f32),
            jax.ShapeDtypeStruct((2 * levels * ny, nx), f32),
        ),
        in_specs=[pl.BlockSpec(memory_space=pltpu.HBM)] * 7,
        out_specs=(vmem, vmem),
        scratch_shapes=list(scratch.values()),
        compiler_params=pltpu.CompilerParams(
            collective_id=0, has_side_effects=True, vmem_limit_bytes=125 * 512 * 1024
        ),
    )(*inputs)
    return p_new.reshape(pressure.shape), u_new.reshape(velocity.shape)


def solution(mesh):
    placed = (
        P(None, None, "py", "px"),
        P(None, "py", "px"),
        P(None, "py", "px"),
        P(None, None, "py", "px"),
        P(None, "py", "px"),
        P(None, None, "py", "px"),
        P(None, "py", "px"),
    )
    return jax.shard_map(
        functools.partial(local, mesh.shape["px"], mesh.shape["py"]),
        mesh=mesh,
        in_specs=placed,
        out_specs=(P(None, "py", "px"), P(None, None, "py", "px")),
        check_vma=False,
    )
```

```python
import functools

import jax
import jax.numpy as jnp
from jax import lax
from jax.experimental import pallas as pl
from jax.experimental.pallas import tpu as pltpu
from jax.sharding import PartitionSpec as P

BLOCK = 4
ITERS = 4
OUTER = 2
SHIFT = 3.0
MESH = pl.DeviceIdType.MESH


def solve(gram, right):
    size = len(right)
    gram = [row[:] for row in gram]
    right = right[:]
    first = [gram[i][i] for i in range(size)]
    inverse = []
    for k in range(size):
        inverse.append(jnp.where(gram[k][k] > 1e-7 * first[k], 1.0 / gram[k][k], 0.0))
        for i in range(k + 1, size):
            factor = gram[k][i] * inverse[k]
            for j in range(i, size):
                gram[i][j] = gram[i][j] - factor * gram[k][j]
            right[i] = right[i] - factor * right[k]
    weights = [None] * size
    for k in reversed(range(size)):
        total = right[k]
        for j in range(k + 1, size):
            total = total - gram[k][j] * weights[j]
        weights[k] = total * inverse[k]
    return weights


def kernel(
    npx, npy, ny, nb, nx,
    vel_hbm, pres_hbm, mass_hbm, face_hbm, vert_hbm, inv_hbm, orient_hbm,
    p_out, u_out,
    vel_ref, pres_ref, mass_ref, face_ref, vert_ref, inv_ref, orient_ref,
    wide, wide_w, mass, ce, cw, cn, cs, wu, wl, xc, binv, prs, fe, fn, res, G, MG, gs, gn, gpk, gxw, gxe,
    W, V, low_p, seam, hs, hn, hs0, pk, xw, xe, pk0, xw0, red, edges, pkC, hnC, hsC, xwC, xeC, cornersC, xcH, ends, hnD, xeD, cornersD,
    send_h, recv_h, send_r, recv_r, fetch,
):
    levels = BLOCK * nb
    tiles = levels // 8
    count = npx * npy
    px, py = lax.axis_index("px"), lax.axis_index("py")
    east, west = lax.rem(px + 1, npx), lax.rem(px + npx - 1, npx)
    has_north, has_south = py < npy - 1, py > 0
    me = px * npy + py

    barrier = pltpu.get_barrier_semaphore()

    partners = [
        (lax.rem(px + i, npx), lax.rem(py + j, npy))
        for i in range(npx) for j in range(npy) if i or j
    ]
    for target in partners:
        pl.semaphore_signal(barrier, inc=1, device_id=target, device_id_type=MESH)

    fetches = [
        pltpu.make_async_copy(src, dst, fetch.at[n])
        for n, (src, dst) in enumerate([
            (face_hbm, face_ref), (pres_hbm, pres_ref), (vel_hbm, vel_ref), (orient_hbm, orient_ref),
            (mass_hbm, mass_ref), (vert_hbm, vert_ref), (inv_hbm, inv_ref),
        ])
    ]
    for copy in fetches:
        copy.start()

    def gather(ref, base, y):
        return jnp.concatenate(
            [
                ref[pl.ds(base + m * ny + y, nb, stride=BLOCK * ny), :]
                for m in range(BLOCK)
            ],
            axis=0,
        )

    def scatter(ref, base, y, value):
        for m in range(BLOCK):
            ref[pl.ds(base + m * ny + y, nb, stride=BLOCK * ny), :] = value[m * nb : (m + 1) * nb]

    lane = lax.broadcasted_iota(jnp.int32, (8, nx), 1)
    lane_l = lax.broadcasted_iota(jnp.int32, (levels, nx), 1)
    even = lax.rem(lane, 2) == 0
    lane_16 = lax.broadcasted_iota(jnp.int32, (16, nx), 1)
    group = lax.broadcasted_iota(jnp.int32, (16, nx), 0)

    def pack(slabs):
        total = jnp.zeros((8, nx), jnp.float32)
        for y in range(ny):
            for t in range(tiles):
                i = y * tiles + t
                turned = slabs[y][t * 8 : (t + 1) * 8]
                if i:
                    turned = pltpu.roll(turned, 2 * i, axis=1)
                mine = (lane == 2 * i) | (lane == (2 * i - 1) % nx)
                total = jnp.where(mine, turned, total)
        return total

    def meet(from_west, from_east):
        return jnp.where(even, pltpu.roll(from_west, 1, axis=1), pltpu.roll(from_east, nx - 1, axis=1))

    def spread(packed, y):
        parts = []
        for t in range(tiles):
            i = y * tiles + t
            parts.append(pltpu.roll(packed, nx - 2 * i, axis=1) if i else packed)
        return jnp.concatenate(parts, axis=0)

    def up(slab):
        return jnp.concatenate([slab[nb:], pltpu.roll(slab[:nb], nb - 1, axis=0)], axis=0)

    def down(slab):
        return jnp.concatenate([pltpu.roll(slab[levels - nb :], 1, axis=0), slab[: levels - nb]], axis=0)

    def roll_w(slab):
        return pltpu.roll(slab, 1, axis=1)

    def roll_e(slab):
        return pltpu.roll(slab, nx - 1, axis=1)

    def remote(src, dst, pair, target, sends=None, lands=None):
        copy = pltpu.make_async_remote_copy(
            src_ref=src, dst_ref=dst, send_sem=pair[0], recv_sem=pair[1],
            device_id=target, device_id_type=MESH)
        return copy, sends, lands

    def sems(k, n):
        return send_h.at[k, n], recv_h.at[k, n]

    def y_copies(low, high, low_dst, high_dst, k):
        return [
            remote(high, high_dst, sems(k, 0), (px, py + 1), has_north, has_south),
            remote(low, low_dst, sems(k, 1), (px, py - 1), has_south, has_north),
        ]

    def x_copies(to_east, to_west, east_dst, west_dst, k):
        return [
            remote(to_east, east_dst, sems(k, 2), (east, py)),
            remote(to_west, west_dst, sems(k, 3), (west, py)),
        ]

    def corner_copies(src, dst, k):
        return [
            remote(src, dst.at[0], sems(k, 4), (east, py + 1), has_north, has_south),
            remote(src, dst.at[1], sems(k, 5), (west, py + 1), has_north, has_south),
            remote(src, dst.at[2], sems(k, 6), (east, py - 1), has_south, has_north),
            remote(src, dst.at[3], sems(k, 7), (west, py - 1), has_south, has_north),
        ]

    def under(condition, action):
        if condition is None:
            action()
        else:
            pl.when(condition)(action)

    def start(copies):
        for copy, sends, _ in copies:
            under(sends, copy.start)

    def finish(copies):
        for copy, _, lands in copies:
            under(lands, copy.wait_recv)

    def sent(copies):
        for copy, sends, _ in copies:
            under(sends, copy.wait_send)

    place = lax.div(lax.rem(lane + 1, nx), 2)
    lane_row = lax.div(place, tiles)
    member = lax.div(lax.rem(place, tiles), tiles // BLOCK)
    reach = 2 * tiles * (ny - 1)

    def corners(slots):
        south = jnp.where(
            even, pltpu.roll(slots[0], nx - reach + 1, axis=1), pltpu.roll(slots[1], nx - reach - 1, axis=1))
        north = jnp.where(
            even, pltpu.roll(slots[2], reach + 1, axis=1), pltpu.roll(slots[3], reach - 1, axis=1))
        return jnp.where(lane_row == ny - 1, north, jnp.where(lane_row == 0, south, 0.0))

    def precondition_packed(value):
        step = 2 * (tiles // BLOCK)
        turned = {
            d: pltpu.roll(value, (step * d) % nx, axis=1) if d else value
            for d in range(1 - BLOCK, BLOCK)
        }
        total = jnp.zeros_like(value)
        for j in range(BLOCK):
            brought = turned[-j]
            for m in range(1, BLOCK):
                brought = jnp.where(member == m, turned[m - j], brought)
            total += meet(xwC[2 + j], xeC[2 + j]) * brought
        return total

    def precondition_rows(entries, blocks):
        parts = []
        for m in range(BLOCK):
            rows = slice(m * nb, (m + 1) * nb)
            parts.append(sum(entries[1 + j, rows] * blocks[j * nb : (j + 1) * nb] for j in range(BLOCK)))
        return jnp.concatenate(parts, axis=0)

    for copy in fetches[:4]:
        copy.wait()
    wide[0] = face_ref[0 : levels * ny].astype(jnp.float32)
    wide[1] = face_ref[levels * ny :].astype(jnp.float32)
    sign = 2.0 * orient_ref[...].astype(jnp.float32) - 1.0
    for y in range(ny):
        ce[y] = gather(wide.at[0], 0, y)
        cn[y] = gather(wide.at[1], 0, y)
        prs[y] = gather(pres_ref, 0, y)
        fe[y] = sign[y : y + 1] * gather(vel_ref, 0, y)
        fn[y] = sign[ny + y : ny + y + 1] * gather(vel_ref, levels * ny, y)
    seam[0] = prs[ny - 1]
    low_p[...] = prs[0]
    seam[1] = fn[ny - 1]
    seam[2] = cn[ny - 1]
    pk0[0] = pack(prs)
    pk0[1] = pack(fe)
    pk0[2] = pack(ce)

    @pl.when(jnp.logical_not(has_south))
    def _():
        hs0[...] = jnp.zeros_like(hs0)
        hs[...] = jnp.zeros_like(hs)
        hsC[...] = jnp.zeros_like(hsC)
        cornersC[0:2] = jnp.zeros_like(cornersC[0:2])
        cornersD[:, 0:2] = jnp.zeros_like(cornersD[:, 0:2])
        gs[...] = jnp.zeros_like(gs)

    @pl.when(jnp.logical_not(has_north))
    def _():
        hn[...] = jnp.zeros_like(hn)
        hnD[...] = jnp.zeros_like(hnD)
        hnC[...] = jnp.zeros_like(hnC)
        cornersC[2:4] = jnp.zeros_like(cornersC[2:4])
        cornersD[:, 2:4] = jnp.zeros_like(cornersD[:, 2:4])
        gn[...] = jnp.zeros_like(gn)

    pl.semaphore_wait(barrier, count - 1)

    first = y_copies(low_p, seam, hn.at[0], hs0, 0) + x_copies(pk0, pk0.at[0], xw0, xe.at[0], 0)
    start(first)

    for copy in fetches[4:]:
        copy.wait()
    wide[0] = mass_ref[...].astype(jnp.float32)
    wide_w[0 : levels - 1] = vert_ref[...].astype(jnp.float32)
    wide_w[levels - 1] = jnp.zeros((ny, nx), jnp.float32)
    for j in range(BLOCK):
        wide[1 + j] = inv_ref[j * levels * ny : (j + 1) * levels * ny].astype(jnp.float32)
    for y in range(ny):
        mass[y] = gather(wide.at[0], 0, y)
        slab = jnp.concatenate(
            [wide_w[pl.ds(m, nb, stride=BLOCK), y, :] for m in range(BLOCK)], axis=0
        )
        wu[y] = slab
        wl[y] = down(slab)
        for j in range(BLOCK):
            binv[j, y] = gather(wide.at[1 + j], 0, y)

    edges[0, 0], edges[1, 0] = ce[0], ce[ny - 1]
    pkC[0], pkC[1] = pk0[2], pack(cn)
    for j in range(BLOCK):
        edges[0, 1 + j], edges[1, 1 + j] = binv[j, 0], binv[j, ny - 1]
        pkC[2 + j] = pack(binv.at[j])
    beyond = 2 + OUTER * ITERS + ITERS
    fixed = y_copies(edges.at[0], edges.at[1], hnC, hsC, beyond)
    fixed += x_copies(pkC, pkC, xwC, xeC, beyond)
    fixed += corner_copies(pkC.at[pl.ds(0, 2)], cornersC, beyond)
    start(fixed)
    finish(first)
    packed_c = meet(xw0[2], xw0[2])
    packed_f = meet(xw0[1], xw0[1])
    for y in range(ny):
        left = jnp.where(lane_l == 0, spread(packed_c, y), roll_w(ce[y]))
        cw[y] = left
        cs[y] = hs0[2] if y == 0 else cn[y - 1]
        xc[y] = jnp.where(lane_l == 0, left, jnp.where(lane_l == nx - 1, ce[y], 0.0))

    def inside(values, y):
        v = values[y]
        to_east = jnp.where(lane_l == nx - 1, 0.0, roll_e(v))
        to_west = jnp.where(lane_l == 0, 0.0, roll_w(v))
        flat = ce[y] * (v - to_east) + cw[y] * (v - to_west)
        flat += cn[y] * (v - values[y + 1]) if y < ny - 1 else cn[y] * v
        flat += cs[y] * (v - values[y - 1]) if y > 0 else cs[y] * v
        return flat, mass[y] * v + flat + wu[y] * (v - up(v)) + wl[y] * (v - down(v))

    def rim(y, packed, south, north):
        total = xc[y] * spread(packed, y)
        if y == 0:
            total += cs[y] * south
        if y == ny - 1:
            total += cn[y] * north
        return total

    def precondition(blocks, y):
        parts = []
        for m in range(BLOCK):
            rows = slice(m * nb, (m + 1) * nb)
            total = binv[0, y, rows] * blocks[0:nb]
            for j in range(1, BLOCK):
                total += binv[j, y, rows] * blocks[j * nb : (j + 1) * nb]
            parts.append(total)
        return jnp.concatenate(parts, axis=0)

    def fold(slab):
        total = slab[0:8]
        for t in range(1, tiles):
            total += slab[t * 8 : (t + 1) * 8]
        return total

    p_south, p_north = hs0[0], hn[0]
    p_packed = meet(xw0[0], xe[0])

    pending = []

    def offer(n):
        gpk[n] = pack([MG[n, y] for y in range(ny)])
        k = 1 + OUTER * ITERS + n
        copies = y_copies(MG.at[n, 0], MG.at[n, ny - 1], gn.at[n], gs.at[n], k)
        copies += x_copies(gpk.at[n], gpk.at[n], gxw.at[n], gxe.at[n], k)
        start(copies)
        pending.append(copies)
        return copies

    def combine(first, terms, factors):
        for term, factor in zip(terms, factors):
            first += factor * term
        return first

    for y in range(ny):
        f_west = jnp.where(lane_l == 0, spread(packed_f, y), roll_w(fe[y]))
        f_south = hs0[1] if y == 0 else fn[y - 1]
        div = fe[y] - f_west + fn[y] - f_south
        flat, image = inside(prs, y)
        border = rim(y, p_packed, p_south, p_north)
        residual = mass[y] * prs[y] - div - (image - border)
        res[y] = residual
        W[0, y] = precondition(residual, y)
        G[ITERS, y] = residual - (flat - border)

    def update(outer, packs, souths, norths, weights, wide_weights, state):
        p_packed, p_south, p_north = state
        p_packed = combine(p_packed, packs, weights)
        p_south = combine(p_south, souths, wide_weights)
        p_north = combine(p_north, norths, wide_weights)
        for y in range(ny):
            prs[y] = combine(prs[y], [W[outer * ITERS + i, y] for i in range(ITERS)], wide_weights)
        for y in range(ny):
            value = prs[y]
            to_east = jnp.where(lane_l == nx - 1, spread(p_packed, y), roll_e(value))
            to_north = prs[y + 1] if y < ny - 1 else p_north
            fe[y] = fe[y] + ce[y] * (value - to_east)
            fn[y] = fn[y] + cn[y] * (value - to_north)
        return p_packed, p_south, p_north

    state = (p_packed, p_south, p_north)
    late = None
    offers = []
    for outer in range(OUTER):
        start_w = outer * ITERS
        packs, souths, norths = [], [], []
        dots = {}
        todo, terms = [], [ITERS] if outer < OUTER - 1 else []
        derived = started if outer > 0 else None

        def products(i):
            for j in range(i + 1):
                dots[j, i] = sum(fold(V[j, y] * V[i, y]) for y in range(ny))
            dots["r", i] = sum(fold(res[y] * V[i, y]) for y in range(ny))

        for i in range(ITERS):
            k = 1 + outer * ITERS + i
            here = W.at[start_w + i]
            fresh = derived is None
            double = fresh and i < ITERS - 1
            if fresh:
                own = pack([here[y] for y in range(ny)])
                pk[k - 1, 0] = own
            if fresh and not double:
                copies = y_copies(here.at[0], here.at[ny - 1], hn.at[k], hs.at[k - 1, 0], k)
                copies += x_copies(pk.at[k - 1, 0], pk.at[k - 1, 0], xw.at[k - 1, 0], xe.at[k], k)
                start(copies)
            for y in range(ny):
                flat, image = inside(here, y)
                V[i, y] = image
                if outer < OUTER - 1:
                    G[i, y] = mass[y] * here[y] - flat - image
            if double:
                for y in range(ny):
                    W[start_w + i + 1, y] = precondition(V[i, y], y) - SHIFT * here[y]
                ahead = W.at[start_w + i + 1]
                pk[k - 1, 1] = pack([ahead[y] for y in range(ny)])
                for n, y in enumerate((0, ny - 1)):
                    ends[k - 1, n, 0], ends[k - 1, n, 1] = here[y], ahead[y]
                copies = y_copies(ends.at[k - 1, 0], ends.at[k - 1, 1], hnD.at[k - 1], hs.at[k - 1], k)
                copies += x_copies(pk.at[k - 1], pk.at[k - 1], xw.at[k - 1], xeD.at[k - 1], k)
                copies += corner_copies(pk.at[k - 1, 0], cornersD.at[k - 1], k)
                start(copies)
            if fresh:
                pending.append(copies)
                for n in todo:
                    products(n)
                todo = []
                for n in terms:
                    for y in range(ny):
                        MG[n, y] = precondition(G[n, y], y)
                    offers.append((n, offer(n)))
                terms = []
                if late is not None:
                    state = update(outer - 1, *late, state)
                    late = None
                finish(copies)
                south = hs[k - 1, 0]
                north = hnD[k - 1, 0] if double else hn[k]
                packed = meet(xw[k - 1, 0], xeD[k - 1, 0] if double else xe[k])
            else:
                packed, south, north = derived
            derived = None
            if double:
                if fixed is not None:
                    finish(fixed)
                    pending.append(fixed)
                    fixed = None
                    coef = corners([cornersC[n, 0] for n in range(4)])
                    for n, entries, row in ((0, hsC, 0), (1, hnC, ny - 1)):
                        xcH[n] = jnp.where(
                            lane_l == 0, spread(coef, row), jnp.where(lane_l == nx - 1, entries[0], 0.0))
                    inner = jnp.where(even, packed_c, pk0[2])
                    outward = jnp.where(
                        lane_row == 0, corners([cornersC[n, 1] for n in range(4)]),
                        jnp.where(lane_row == ny - 1, meet(xwC[1], xeC[1]), 0.0))
                corner = corners([cornersD[k - 1, n] for n in range(4)])
                derived = (
                    meet(xw[k - 1, 1], xeD[k - 1, 1]) - precondition_packed(inner * own + outward * corner),
                    hs[k - 1, 1] - precondition_rows(hsC, xcH[0] * spread(corner, 0) + cs[0] * here[0]),
                    hnD[k - 1, 1] - precondition_rows(
                        hnC, xcH[1] * spread(corner, ny - 1) + cn[ny - 1] * here[ny - 1]),
                )
            packs.append(packed)
            souths.append(south)
            norths.append(north)
            for y in range(ny):
                border = rim(y, packed, south, north)
                image = V[i, y] - border
                V[i, y] = image
                if i < ITERS - 1:
                    W[start_w + i + 1, y] = precondition(image, y) - SHIFT * here[y]
                if outer < OUTER - 1:
                    G[i, y] = G[i, y] + 2.0 * border
            todo.append(i)
            if outer < OUTER - 1:
                terms.append(i)
        for n in todo:
            products(n)

        order = [(j, i) for i in range(ITERS) for j in range(i + 1)]
        order += [("r", i) for i in range(ITERS)]
        rows = [jnp.sum(dots[key], axis=0, keepdims=True) for key in order]
        rows += [jnp.zeros_like(rows[0])] * (16 - len(rows))
        rows = jnp.sum(jnp.concatenate(rows, axis=0), axis=1, keepdims=True)
        red[outer, me] = jnp.sum(jnp.where(group == lane_16, rows, 0.0), axis=0, keepdims=True)
        for target in partners:
            pltpu.make_async_remote_copy(
                src_ref=red.at[outer, me], dst_ref=red.at[outer, me],
                send_sem=send_r.at[outer], recv_sem=recv_r.at[outer],
                device_id=target, device_id_type=MESH).start()
        if outer < OUTER - 1:
            for n in terms:
                for y in range(ny):
                    MG[n, y] = precondition(G[n, y], y)
                offers.append((n, offer(n)))
        rest = red.at[outer, pl.ds(0, count - 1)]
        pltpu.make_async_copy(rest, rest, recv_r.at[outer]).wait()
        total = jnp.sum(red[outer], axis=0)
        column = jnp.sum(jnp.where(group == lane_16, total, 0.0), axis=1, keepdims=True)
        sums = {}
        for n, key in enumerate(order):
            sums[key] = jnp.broadcast_to(column[n : n + 1], (8, nx))
        gram = [[sums[min(i, j), max(i, j)] for j in range(ITERS)] for i in range(ITERS)]
        weights = solve(gram, [sums["r", i] for i in range(ITERS)])
        wide_weights = [jnp.broadcast_to(c[0:1], (levels, nx)) for c in weights]

        late = (packs, souths, norths, weights, wide_weights)
        if outer < OUTER - 1:
            for y in range(ny):
                W[start_w + ITERS, y] = combine(MG[ITERS, y], [MG[i, y] for i in range(ITERS)], wide_weights)
                res[y] = combine(G[ITERS, y], [G[i, y] for i in range(ITERS)], wide_weights)
            for term, copies in offers:
                finish(copies)
            offers = []
            meets = [meet(gxw[i], gxe[i]) for i in range(ITERS + 1)]
            started = (
                combine(meets[ITERS], meets[:ITERS], weights),
                combine(gs[ITERS], [gs[i] for i in range(ITERS)], wide_weights),
                combine(gn[ITERS], [gn[i] for i in range(ITERS)], wide_weights),
            )
    update(OUTER - 1, *late, state)
    for y in range(ny):
        scatter(p_out, 0, y, prs[y])
        scatter(u_out, 0, y, sign[y : y + 1] * fe[y])
        scatter(u_out, levels * ny, y, sign[ny + y : ny + y + 1] * fn[y])
    sent(first)
    for copies in pending:
        sent(copies)
    for outer in range(OUTER):
        rest = red.at[outer, pl.ds(0, count - 1)]
        pltpu.make_async_copy(rest, rest, send_r.at[outer]).wait()


def local(npx, npy, velocity, pressure, mass, face_coeff, vert_coeff, block_inverse, orientation):
    levels, ny, nx = pressure.shape
    nb = levels // BLOCK
    f32 = jnp.float32
    rounds = OUTER * ITERS
    field = pltpu.VMEM((ny, levels, nx), f32)
    slab = pltpu.VMEM((levels, nx), f32)
    flat = [a.reshape(-1, nx) for a in (velocity, pressure, mass, face_coeff, block_inverse, orientation)]
    inputs = flat[:4] + [vert_coeff] + flat[4:]
    names = ("vel_ref", "pres_ref", "mass_ref", "face_ref", "vert_ref", "inv_ref", "orient_ref")
    vmem = pl.BlockSpec(memory_space=pltpu.VMEM)
    scratch = dict(
        **{name: pltpu.VMEM(a.shape, a.dtype) for name, a in zip(names, inputs)},
        wide=pltpu.VMEM((1 + BLOCK, levels * ny, nx), f32),
        wide_w=pltpu.VMEM((levels, ny, nx), f32),
        mass=field, ce=field, cw=field, cn=field, cs=field, wu=field, wl=field, xc=field,
        binv=pltpu.VMEM((BLOCK, ny, levels, nx), f32),
        prs=field, fe=field, fn=field, res=field,
        G=pltpu.VMEM((ITERS + 1, ny, levels, nx), f32),
        MG=pltpu.VMEM((ITERS + 1, ny, levels, nx), f32),
        gs=pltpu.VMEM((ITERS + 1, levels, nx), f32),
        gn=pltpu.VMEM((ITERS + 1, levels, nx), f32),
        gpk=pltpu.VMEM((ITERS + 1, 8, nx), f32),
        gxw=pltpu.VMEM((ITERS + 1, 8, nx), f32),
        gxe=pltpu.VMEM((ITERS + 1, 8, nx), f32),
        W=pltpu.VMEM((OUTER * ITERS, ny, levels, nx), f32),
        V=pltpu.VMEM((ITERS, ny, levels, nx), f32),
        low_p=slab,
        seam=pltpu.VMEM((3, levels, nx), f32),
        hs=pltpu.VMEM((rounds, 2, levels, nx), f32),
        hn=pltpu.VMEM((rounds + 1, levels, nx), f32),
        hs0=pltpu.VMEM((3, levels, nx), f32),
        pk=pltpu.VMEM((rounds, 2, 8, nx), f32),
        xw=pltpu.VMEM((rounds, 2, 8, nx), f32),
        xe=pltpu.VMEM((rounds + 1, 8, nx), f32),
        pk0=pltpu.VMEM((3, 8, nx), f32),
        xw0=pltpu.VMEM((3, 8, nx), f32),
        red=pltpu.VMEM((OUTER, npx * npy, 1, nx), f32),
        edges=pltpu.VMEM((2, 1 + BLOCK, levels, nx), f32),
        pkC=pltpu.VMEM((2 + BLOCK, 8, nx), f32),
        hnC=pltpu.VMEM((1 + BLOCK, levels, nx), f32),
        hsC=pltpu.VMEM((1 + BLOCK, levels, nx), f32),
        xwC=pltpu.VMEM((2 + BLOCK, 8, nx), f32),
        xeC=pltpu.VMEM((2 + BLOCK, 8, nx), f32),
        cornersC=pltpu.VMEM((4, 2, 8, nx), f32),
        xcH=pltpu.VMEM((2, levels, nx), f32),
        ends=pltpu.VMEM((rounds, 2, 2, levels, nx), f32),
        hnD=pltpu.VMEM((rounds, 2, levels, nx), f32),
        xeD=pltpu.VMEM((rounds, 2, 8, nx), f32),
        cornersD=pltpu.VMEM((rounds, 4, 8, nx), f32),
        send_h=pltpu.SemaphoreType.DMA((rounds + ITERS + 3, 8)),
        recv_h=pltpu.SemaphoreType.DMA((rounds + ITERS + 3, 8)),
        send_r=pltpu.SemaphoreType.DMA((OUTER,)),
        recv_r=pltpu.SemaphoreType.DMA((OUTER,)),
        fetch=pltpu.SemaphoreType.DMA((7,)),
    )
    p_new, u_new = pl.pallas_call(
        functools.partial(kernel, npx, npy, ny, nb, nx),
        out_shape=(
            jax.ShapeDtypeStruct((levels * ny, nx), f32),
            jax.ShapeDtypeStruct((2 * levels * ny, nx), f32),
        ),
        in_specs=[pl.BlockSpec(memory_space=pltpu.HBM)] * 7,
        out_specs=(vmem, vmem),
        scratch_shapes=list(scratch.values()),
        compiler_params=pltpu.CompilerParams(
            collective_id=0, has_side_effects=True, vmem_limit_bytes=125 * 512 * 1024
        ),
    )(*inputs)
    return p_new.reshape(pressure.shape), u_new.reshape(velocity.shape)


def solution(mesh):
    placed = (
        P(None, None, "py", "px"),
        P(None, "py", "px"),
        P(None, "py", "px"),
        P(None, None, "py", "px"),
        P(None, "py", "px"),
        P(None, None, "py", "px"),
        P(None, "py", "px"),
    )
    return jax.shard_map(
        functools.partial(local, mesh.shape["px"], mesh.shape["py"]),
        mesh=mesh,
        in_specs=placed,
        out_specs=(P(None, "py", "px"), P(None, None, "py", "px")),
        check_vma=False,
    )
```
